32 devices in a mesh: seq: 16 (over z, x, core), head: 2 (over y).
Axes of the slice: x: 2, y: 2, z: 4, core: 2. Of those that a mesh axis runs over, the one named last changes fastest.
Arguments:
- queries: bfloat16 [4096, 32, 128], P('seq', 'head'), may hold values from -36 to 36
- keys: bfloat16 [4096, 16, 128], P('seq', 'head'), may hold values from -4 to 4
- values: bfloat16 [4096, 16, 128], P('seq', 'head'), may hold values from -12 to 12
- output_gradient: bfloat16 [4096, 32, 128], P('seq', 'head'), may hold values from -6 to 6
- segment_ids: int32 [4096], P('seq'), may hold values from 0 to 3, never falling along the last dimension, each value on 1 to 2048 neighbouring positions
- block_order: int32 [32], replicated, may hold values from 0 to 31, each once
Outputs:
- relaid: bfloat16 [4096, 4096], P(('seq', 'head'))
- query_grad: bfloat16 [4096, 32, 128], P('seq', 'head')
- key_grad: bfloat16 [4096, 16, 128], P('seq', 'head')
- value_grad: bfloat16 [4096, 16, 128], P('seq', 'head')
The draws below stay inside these ranges and needn't reach their ends.
Inputs may be any that keep to these rules, and one draw needn't show every extreme that they name: `segment_ids`: segment ids never fall along the sequence; each document holds 1 to 2048 positions and one holds exactly 2048. `block_order`: each block number appears exactly once.
All inputs are finite; a program needn't handle non-finite values.
Results may differ from the reference program's by a relative error of at most 0.013.
Values may be sent and summed in bfloat16 or wider, within the bound.
A program may use at most 128 MiB of HBM per device.

```python
import math
import jax
import jax.numpy as jnp
import numpy as np
from jax import lax

QUERY_HEADS = 32
KEY_VALUE_HEADS = 16
HEAD_DIM = 128
WINDOW_LENGTH = 1024
QSCALAR = 168
SEQUENCE_TOKENS = 4096
BLK = 128
NBLK = 32
SEGMENTS = 4
SEG_MOST = 2048


def draw_keys(key, part):
    final_output = jax.random.truncated_normal(jax.random.fold_in(key, 105), -4.0, 4.0, (SEQUENCE_TOKENS, KEY_VALUE_HEADS, HEAD_DIM), jnp.float32)
    return final_output.astype(jnp.bfloat16)


def draw_queries(key, part):
    final_output = jax.random.truncated_normal(jax.random.fold_in(key, 107), -6.0, 6.0, (SEQUENCE_TOKENS, QUERY_HEADS, HEAD_DIM), jnp.float32)
    return final_output.astype(jnp.bfloat16)


def shard_levels(rng, dims, shards, smallest, largest):
    gain = 1.0
    for axis_at, shards_of in shards:
        heights = jax.random.uniform(jax.random.fold_in(jax.random.fold_in(rng, 6), axis_at), (shards_of,), jnp.float32, smallest / len(shards), largest / len(shards))
        gain = gain * jnp.repeat(jnp.exp(heights), dims[axis_at] // shards_of).reshape((-1,) + (1,) * (len(dims) - 1 - axis_at))
    return gain


def split_up(number_of, total, most, lean):
    weights = [(1 << 20) // math.isqrt(rank ** lean) + 1 for rank in range(2, number_of + 1)]
    spare, counts = total - most - (number_of - 1), [1] * (number_of - 1)
    while spare > 0:
        movable = [i for i in range(number_of - 1) if counts[i] < most]
        mass, budget = sum([weights[i] for i in movable]), spare
        for i in movable:
            extra = min(most - counts[i], max(1, budget * weights[i] // mass), spare)
            counts[i] = counts[i] + extra
            spare = spare - extra
    return np.array([most] + counts)


def ragged(rng, amount, total, reach, skew):
    if amount == 2:
        one = jax.random.randint(rng, (), max(1, total - reach), min(reach, total - 1) + 1)
        return jnp.stack([one, total - one])
    lengths = jnp.asarray(split_up(amount, total, reach, skew), jnp.int32)
    pairs = (amount - 1) // 2
    donor, sink = lengths[1:1 + 2 * pairs:2], lengths[2:2 + 2 * pairs:2]
    slack = jnp.minimum(donor - 1, reach - sink)
    moved = jax.random.randint(jax.random.fold_in(rng, 1), (pairs,), 0, 1 << 20) % (slack + 1)
    lengths = lengths.at[1:1 + 2 * pairs:2].set(donor - moved).at[2:2 + 2 * pairs:2].set(sink + moved)
    return lengths[jax.random.permutation(jax.random.fold_in(rng, 2), amount)]


def bell_draw(own_key, extent, spread, reach, shards=(), held_as=jnp.bfloat16):
    values = jax.random.normal(own_key, extent, jnp.float32) * spread
    if len(shards) > 0:
        values = shard_levels(own_key, extent, shards, -0.22, 0.18) * values
    return jnp.clip(values, min=-reach, max=reach).astype(held_as)


def setup_inputs(seed: int = 0) -> dict:
    arg_keys = jax.random.split(jax.random.key(seed), 7)
    queries = draw_queries(jax.random.fold_in(arg_keys[6], 71), 0)
    keys = draw_keys(jax.random.fold_in(arg_keys[6], 71), 0)
    values = bell_draw(arg_keys[2], (SEQUENCE_TOKENS, KEY_VALUE_HEADS, HEAD_DIM), 3.0, 12.0, ((0, 16), (1, 2)))
    output_gradient = bell_draw(arg_keys[3], (SEQUENCE_TOKENS, QUERY_HEADS, HEAD_DIM), 1.0, 6.0, ((0, 16), (1, 2)))
    segment_ids = jnp.searchsorted(jnp.cumsum(ragged(arg_keys[4], SEGMENTS, SEQUENCE_TOKENS, SEG_MOST, 1)), jnp.arange(SEQUENCE_TOKENS), side="right").astype(jnp.int32)
    block_order = jax.random.permutation(arg_keys[5], NBLK).astype(jnp.int32)
    return {"queries": queries, "keys": keys, "values": values, "output_gradient": output_gradient, "segment_ids": segment_ids, "block_order": block_order}


def reference(queries, keys, values, output_gradient, segment_ids, block_order):
    factor = QSCALAR ** -0.5
    number_rows = 256
    key_span = WINDOW_LENGTH + number_rows
    blocks = SEQUENCE_TOKENS // number_rows
    group_width = QUERY_HEADS // KEY_VALUE_HEADS
    padded_keys = jnp.concatenate([jnp.zeros((WINDOW_LENGTH, KEY_VALUE_HEADS, HEAD_DIM), keys.dtype), keys], axis=0)
    padded_values = jnp.concatenate([jnp.zeros((WINDOW_LENGTH, KEY_VALUE_HEADS, HEAD_DIM), values.dtype), values], axis=0)
    segs_pad = jnp.concatenate([jnp.full((WINDOW_LENGTH,), -1, jnp.int32), segment_ids.astype(jnp.int32)])

    def one_block(totals, block_index):
        key_acc, value_acc = totals
        leading_row = (block_index * number_rows).astype(jnp.int32)
        query_tile_rows = lax.dynamic_slice_in_dim(queries, leading_row, number_rows, 0).astype(jnp.float32).reshape(number_rows, KEY_VALUE_HEADS, group_width, HEAD_DIM)
        gradient_block = lax.dynamic_slice_in_dim(output_gradient, leading_row, number_rows, 0).astype(jnp.float32).reshape(number_rows, KEY_VALUE_HEADS, group_width, HEAD_DIM)
        key_block = lax.dynamic_slice_in_dim(padded_keys, leading_row, key_span, 0).astype(jnp.float32)
        value_block = lax.dynamic_slice_in_dim(padded_values, leading_row, key_span, 0).astype(jnp.float32)
        query_segs = lax.dynamic_slice_in_dim(segment_ids.astype(jnp.int32), leading_row, number_rows, 0)
        key_segs = lax.dynamic_slice_in_dim(segs_pad, leading_row, key_span, 0)
        query_pos = leading_row + jnp.arange(number_rows, dtype=jnp.int32)
        key_pos = leading_row - WINDOW_LENGTH + jnp.arange(key_span, dtype=jnp.int32)
        distance = query_pos[:, None] - key_pos[None, :]
        allowed = (distance >= 0) & (distance < WINDOW_LENGTH) & (query_segs[:, None] == key_segs[None, :])
        scores = jnp.einsum('tkgd,skd->kgts', query_tile_rows, key_block) * factor
        masked = jnp.where(allowed, scores, -jnp.inf)
        row_max = jnp.max(masked, axis=-1, keepdims=True)
        log_total = row_max + jnp.log(jnp.sum(jnp.exp(masked - row_max), axis=-1, keepdims=True))
        weights = jnp.where(allowed, jnp.exp(scores - log_total), 0.0)
        probs = lax.optimization_barrier(weights.astype(jnp.bfloat16)).astype(jnp.float32)
        attended = jnp.einsum('kgts,skd->tkgd', probs, value_block).astype(jnp.bfloat16)
        delta = jnp.sum(gradient_block * lax.optimization_barrier(attended).astype(jnp.float32), axis=-1)
        dprobs = jnp.einsum('tkgd,skd->kgts', gradient_block, value_block)
        score_grad = weights * (dprobs - jnp.transpose(delta, (1, 2, 0))[..., None])
        score_grad = lax.optimization_barrier(score_grad.astype(jnp.bfloat16)).astype(jnp.float32)
        query_grad = (factor * jnp.einsum('kgts,skd->tkgd', score_grad, key_block)).astype(jnp.bfloat16)
        key_part = factor * jnp.einsum('kgts,tkgd->skd', score_grad, query_tile_rows)
        value_part = jnp.einsum('kgts,tkgd->skd', probs, gradient_block)
        key_acc = lax.dynamic_update_slice_in_dim(key_acc, lax.dynamic_slice_in_dim(key_acc, leading_row, key_span, 0) + key_part, leading_row, 0)
        value_acc = lax.dynamic_update_slice_in_dim(value_acc, lax.dynamic_slice_in_dim(value_acc, leading_row, key_span, 0) + value_part, leading_row, 0)
        return (key_acc, value_acc), (attended.reshape(number_rows, QUERY_HEADS, HEAD_DIM), query_grad.reshape(number_rows, QUERY_HEADS, HEAD_DIM))

    zeroed_total = jnp.zeros((SEQUENCE_TOKENS + WINDOW_LENGTH, KEY_VALUE_HEADS, HEAD_DIM), jnp.float32)
    (key_acc, value_acc), (attended, query_grad) = lax.scan(one_block, (zeroed_total, zeroed_total), jnp.arange(blocks, dtype=jnp.int32))
    attended = attended.reshape(NBLK, BLK, QUERY_HEADS * HEAD_DIM)
    relaid = jnp.take(attended, block_order.astype(jnp.int32), axis=0).reshape(SEQUENCE_TOKENS, QUERY_HEADS * HEAD_DIM)
    query_grad = query_grad.reshape(SEQUENCE_TOKENS, QUERY_HEADS, HEAD_DIM)
    key_grad = key_acc[WINDOW_LENGTH:].astype(jnp.bfloat16)
    value_grad = value_acc[WINDOW_LENGTH:].astype(jnp.bfloat16)
    return (relaid, query_grad, key_grad, value_grad)
```

```python
import functools

import jax
import jax.numpy as jnp
from jax import lax
from jax.experimental import pallas as pl
from jax.experimental.pallas import tpu as pltpu
from jax.sharding import PartitionSpec as P

WINDOW_LENGTH = 1024
QSCALAR = 168
FACTOR = QSCALAR ** (-0.5)
LOG2E = 1.4426950408889634
SEG_ROWS = 16


def shifted(value, axis, by):
    count = lax.axis_size(axis)
    pairs = [(i, i + by) for i in range(count) if 0 <= i + by < count]
    return lax.ppermute(value, axis, pairs)


def dot(a, b, ca, cb):
    return lax.dot_general(a, b, (((ca,), (cb,)), ((), ())), preferred_element_type=jnp.float32)


def attention_kernel(count, *refs):
    q_ref, do_ref, bias_ref = refs[:3]
    k_refs = refs[3 : 3 + count]
    v_refs = refs[3 + count : 3 + 2 * count]
    o_ref, dq_ref = refs[3 + 2 * count : 5 + 2 * count]
    g_refs = refs[5 + 2 * count : 5 + 3 * count]
    p_scr = refs[5 + 3 * count]
    width, tok, dim = q_ref.shape
    rows = width * tok
    q = q_ref[...].reshape(rows, dim)
    do = do_ref[...].reshape(rows, dim)
    top = None
    for b in range(count):
        s = dot(q, k_refs[b][...], 1, 1).reshape(width, tok, tok)
        s = (s + bias_ref[:, b * tok : (b + 1) * tok][None]).reshape(rows, tok)
        p_scr[b] = s
        m = jnp.max(s, axis=1, keepdims=True)
        top = m if top is None else jnp.maximum(top, m)
    total = jnp.zeros((rows, 1), jnp.float32)
    for b in range(count):
        p = jnp.exp2((p_scr[b] - top) * (FACTOR * LOG2E))
        p_scr[b] = p
        total += jnp.sum(p, axis=1, keepdims=True)
    scale = 1.0 / total
    out = jnp.zeros((rows, dim), jnp.float32)
    for b in range(count):
        w = p_scr[b] * scale
        p_scr[b] = w
        probs = w.astype(jnp.bfloat16)
        out += dot(probs, v_refs[b][...], 1, 0)
        g_refs[b][1, 0] = dot(probs, do, 0, 0).astype(g_refs[b].dtype)
    out = out.astype(jnp.bfloat16)
    for w in range(width):
        o_ref[:, w * dim : (w + 1) * dim] = out[w * tok : (w + 1) * tok]
    delta = jnp.sum(do.astype(jnp.float32) * out.astype(jnp.float32), axis=1, keepdims=True)
    dq = jnp.zeros((rows, dim), jnp.float32)
    for b in range(count):
        dp = dot(do, v_refs[b][...], 1, 1)
        ds = (p_scr[b] * (dp - delta)).astype(jnp.bfloat16)
        dq += dot(ds, k_refs[b][...], 1, 0)
        g_refs[b][0, 0] = (FACTOR * dot(ds, q, 0, 0)).astype(g_refs[b].dtype)
    dq_ref[...] = (FACTOR * dq).astype(jnp.bfloat16).reshape(width, tok, dim)


def attention(q, do, bias, windows):
    heads, tok, dim = q.shape
    count = len(windows)
    kv_heads = (windows[0].shape[0] - SEG_ROWS) // (2 * tok)
    width = heads // kv_heads
    head_spec = pl.BlockSpec((width, tok, dim), lambda h: (h, 0, 0))
    key_spec = pl.BlockSpec((tok, dim), lambda h: (h, 0))
    value_spec = pl.BlockSpec((tok, dim), lambda h: (h + kv_heads, 0))
    grad_spec = pl.BlockSpec((2, 1, tok, dim), lambda h: (0, h, 0, 0))
    grad_shape = (2, kv_heads, tok, dim)
    pairs = heads * tok * tok * count
    return pl.pallas_call(
        functools.partial(attention_kernel, count),
        grid=(kv_heads,),
        in_specs=[head_spec, head_spec, pl.BlockSpec((tok, count * tok), lambda h: (0, 0))]
        + [key_spec] * count
        + [value_spec] * count,
        out_specs=[pl.BlockSpec((tok, width * dim), lambda h: (0, h)), head_spec]
        + [grad_spec] * count,
        out_shape=[
            jax.ShapeDtypeStruct((tok, heads * dim), jnp.bfloat16),
            jax.ShapeDtypeStruct((heads, tok, dim), jnp.bfloat16),
        ]
        + [jax.ShapeDtypeStruct(grad_shape, jnp.bfloat16)] * (count - 1)
        + [jax.ShapeDtypeStruct(grad_shape, jnp.float32)],
        scratch_shapes=[pltpu.VMEM((count, width * tok, tok), jnp.float32)],
        compiler_params=pltpu.CompilerParams(vmem_limit_bytes=40 * 2**20),
        cost_estimate=pl.CostEstimate(
            flops=10 * pairs * dim, bytes_accessed=12 * 2**20, transcendentals=pairs
        ),
        name="attention",
    )(q, do, bias, *windows, *windows)


def pick_kernel(order_ref, held_ref, out_ref):
    for q in range(out_ref.shape[0]):
        out_ref[q] = held_ref[order_ref[q]]


def pick(held, order):
    return pl.pallas_call(
        pick_kernel,
        in_specs=[
            pl.BlockSpec(memory_space=pltpu.SMEM),
            pl.BlockSpec(memory_space=pltpu.VMEM),
        ],
        out_specs=pl.BlockSpec(memory_space=pltpu.VMEM),
        out_shape=jax.ShapeDtypeStruct(held.shape, held.dtype),
        name="pick",
    )(order, held)


def local(queries, keys, values, output_gradient, segment_ids, block_order):
    tok, q_heads, dim = queries.shape
    kv_heads = keys.shape[1]
    seq_count = lax.axis_size("seq")
    head_count = lax.axis_size("head")
    reach = (WINDOW_LENGTH - 1) // tok + 1
    anchor = lax.axis_index("seq") * tok

    seg_rows = segment_ids.astype(jnp.bfloat16).reshape(tok // dim, dim)
    own = jnp.concatenate(
        [
            jnp.moveaxis(keys, 1, 0).reshape(kv_heads * tok, dim),
            jnp.moveaxis(values, 1, 0).reshape(kv_heads * tok, dim),
            jnp.pad(seg_rows, ((0, SEG_ROWS - tok // dim), (0, 0))),
        ]
    )
    windows = [shifted(own, "seq", d) for d in range(reach, 0, -1)] + [own]
    base = 2 * kv_heads * tok
    key_segs = jnp.concatenate([w[base : base + tok // dim].reshape(tok) for w in windows])
    query_pos = anchor + jnp.arange(tok, dtype=jnp.int32)
    key_pos = anchor - reach * tok + jnp.arange((reach + 1) * tok, dtype=jnp.int32)
    distance = query_pos[:, None] - key_pos[None, :]
    allowed = (
        (distance >= 0)
        & (distance < WINDOW_LENGTH)
        & (key_pos[None, :] >= 0)
        & (segment_ids.astype(jnp.bfloat16)[:, None] == key_segs[None, :])
    )
    bias = jnp.where(allowed, 0.0, -jnp.inf).astype(jnp.float32)

    attended, dq, *grads = attention(
        jnp.moveaxis(queries, 1, 0), jnp.moveaxis(output_gradient, 1, 0), bias, windows
    )

    nb = block_order.shape[0] // seq_count
    piece = tok // nb // seq_count
    features = q_heads * dim
    flat = jnp.swapaxes(attended.reshape(nb, seq_count, piece, features), 0, 1)
    spread = lax.all_to_all(flat, "seq", split_axis=0, concat_axis=0, tiled=True)
    ordered = pick(spread.reshape(nb * seq_count, piece, features), block_order)
    delivered = lax.all_to_all(
        ordered.reshape(seq_count, nb, piece, features),
        "seq",
        split_axis=0,
        concat_axis=0,
        tiled=True,
    )
    reordered = jnp.swapaxes(delivered, 0, 1).reshape(head_count, tok // head_count, features)
    halves = lax.all_to_all(reordered, "head", split_axis=0, concat_axis=0, tiled=True)
    relaid = jnp.swapaxes(halves, 0, 1).reshape(tok // head_count, head_count * features)

    total = grads[reach]
    for d in range(1, reach + 1):
        total = total + shifted(grads[reach - d], "seq", -d).astype(jnp.float32)
    total = jnp.swapaxes(total, 1, 2).astype(jnp.bfloat16)
    return (relaid, jnp.moveaxis(dq, 0, 1), total[0], total[1])


def solution(mesh):
    placed = (
        P("seq", "head", None),
        P("seq", "head", None),
        P("seq", "head", None),
        P("seq", "head", None),
        P("seq"),
        P(),
    )
    return jax.shard_map(
        local,
        mesh=mesh,
        in_specs=placed,
        out_specs=(
            P(("seq", "head"), None),
            P("seq", "head", None),
            P("seq", "head", None),
            P("seq", "head", None),
        ),
        check_vma=False,
    )
```

```python
import functools

import jax
import jax.numpy as jnp
from jax import lax
from jax.experimental import pallas as pl
from jax.experimental.pallas import tpu as pltpu
from jax.sharding import PartitionSpec as P

WINDOW_LENGTH = 1024
QSCALAR = 168
FACTOR = QSCALAR ** (-0.5)
LOG2E = 1.4426950408889634
SEG_ROWS = 16
MESH = pl.DeviceIdType.MESH


def dot(a, b, ca, cb):
    return lax.dot_general(a, b, (((ca,), (cb,)), ((), ())), preferred_element_type=jnp.float32)


def attention_kernel(
    n_seq,
    q_ref,
    do_ref,
    seg_ref,
    own_ref,
    o_ref,
    dq_ref,
    g_ref,
    kv_in,
    p_scr,
    bias,
    g_x,
    g_z,
    g_own,
    g_out,
    g_in,
    send,
    recv,
    g_send,
    g_recv,
):
    heads, rows_kv, dim = own_ref.shape
    tok = seg_ref.shape[0]
    width = q_ref.shape[0] // heads
    rows = width * tok
    me = lax.axis_index("seq")
    core = lax.rem(me, 2)
    half = lax.rem(me // 2, 2)
    plane = me // 4
    planes = n_seq // 4
    core_peer = me + 1 - 2 * core
    x_peer = me + 2 - 4 * half
    has_prev = plane > 0
    has_next = plane < planes - 1
    Z, X, C, D = 0, 1, 2, 3

    barrier = pltpu.get_barrier_semaphore()

    def greet(who):
        pl.semaphore_signal(barrier, inc=1, device_id={"seq": who}, device_id_type=MESH)

    greet(core_peer)
    greet(x_peer)

    @pl.when(has_prev)
    def _():
        greet(me - 4)

    @pl.when(has_next)
    def _():
        greet(me + 4)

    pl.semaphore_wait(barrier, 2 + has_prev.astype(jnp.int32) + has_next.astype(jnp.int32))

    def copy(kind, h, src, who):
        return pltpu.make_async_remote_copy(
            src_ref=src,
            dst_ref=kv_in.at[kind, h],
            send_sem=send.at[kind, h],
            recv_sem=recv.at[kind, h],
            device_id={"seq": who},
            device_id_type=MESH,
        )

    def z_copy(h):
        return copy(Z, h, own_ref.at[h], me + 4)

    def x_copy(h, src):
        return copy(X, h, src.at[h], x_peer)

    def c_copy(h, src):
        return copy(C, h, src.at[h], core_peer)

    def d_copy(h):
        return copy(D, h, kv_in.at[X, h], core_peer)

    @pl.loop(0, heads)
    def _(h):
        @pl.when(has_next)
        def _():
            z_copy(h).start()

        @pl.when(half == 0)
        def _():
            x_copy(h, own_ref).start()

        @pl.when(core == 0)
        def _():
            c_copy(h, own_ref).start()

        @pl.when(jnp.logical_not(has_prev))
        def _():
            kv_in[Z, h] = jnp.zeros((rows_kv, dim), jnp.bfloat16)

    def stage_z(h):
        @pl.when(has_prev)
        def _():
            copy(Z, h, own_ref.at[h], me - 4).wait_recv()

        @pl.when(half == 1)
        def _():
            x_copy(h, kv_in.at[Z]).start()

        @pl.when(core == 1)
        def _():
            c_copy(h, kv_in.at[Z]).start()

    def stage_x(h):
        x_copy(h, own_ref).wait_recv()
        d_copy(h).start()

    def stage_c(h):
        c_copy(h, own_ref).wait_recv()
        d_copy(h).wait_recv()

    def gcopy(kind, h, who):
        return pltpu.make_async_remote_copy(
            src_ref=g_out.at[kind, h],
            dst_ref=g_in.at[kind, h],
            send_sem=g_send.at[kind, h],
            recv_sem=g_recv.at[kind, h],
            device_id={"seq": who},
            device_id_type=MESH,
        )

    def grad_x(h):
        gcopy(D, h, core_peer).wait_recv()
        total = g_x[h] + g_in[D, h].astype(jnp.float32)
        g_out[X, h] = total.astype(jnp.bfloat16)
        gcopy(X, h, x_peer).start()

    def grad_z(h):
        gcopy(C, h, core_peer).wait_recv()
        gcopy(X, h, x_peer).wait_recv()
        from_c = g_in[C, h].astype(jnp.float32)
        from_x = g_in[X, h].astype(jnp.float32)
        zero = jnp.zeros_like(from_c)
        back = g_z[h] + jnp.where(core == 1, from_c, zero) + jnp.where(half == 1, from_x, zero)
        g_out[Z, h] = back.astype(jnp.bfloat16)
        g_own[h] = g_own[h] + jnp.where(core == 0, from_c, zero) + jnp.where(half == 0, from_x, zero)

        @pl.when(has_prev)
        def _():
            gcopy(Z, h, me - 4).start()

    def finish(h):
        @pl.when(has_next)
        def _():
            gcopy(Z, h, me + 4).wait_recv()
            g_ref[h] = (g_own[h] + g_in[Z, h].astype(jnp.float32)).astype(jnp.bfloat16)

        @pl.when(jnp.logical_not(has_next))
        def _():
            g_ref[h] = g_own[h].astype(jnp.bfloat16)

    spans = (4, 2, 3 - 2 * core, 1 + 2 * core, 0)

    def chunk(b, h):
        return own_ref.at[h] if b == 4 else kv_in.at[b, h]

    def masks():
        gap = lax.broadcasted_iota(jnp.int32, (tok, tok), 0) - lax.broadcasted_iota(
            jnp.int32, (tok, tok), 1
        )
        seg_q = seg_ref[...]
        for b in range(5):
            segs = chunk(b, 0)[2 * tok :, :].astype(jnp.float32)
            seg_k = jnp.concatenate([segs[r : r + 1] for r in range(tok // dim)], axis=1)
            far = gap + spans[b] * tok
            near = jnp.where(me >= spans[b], WINDOW_LENGTH, -1)
            allowed = (far >= 0) & (far < near) & (seg_q == seg_k)
            bias[b] = jnp.where(allowed, 0.0, -jnp.inf)

    def compute(h):
        q = q_ref[pl.ds(h * width, width)].reshape(rows, dim)
        do = do_ref[pl.ds(h * width, width)].reshape(rows, dim)
        top = None
        for b in range(5):
            s = dot(q, chunk(b, h)[:tok, :], 1, 1).reshape(width, tok, tok)
            s = (s + bias[b][None]).reshape(rows, tok)
            p_scr[b] = s
            m = jnp.max(s, axis=1, keepdims=True)
            top = m if top is None else jnp.maximum(top, m)
        total = jnp.zeros((rows, 1), jnp.float32)
        for b in range(5):
            p = jnp.exp2((p_scr[b] - top) * (FACTOR * LOG2E))
            p_scr[b] = p
            total += jnp.sum(p, axis=1, keepdims=True)
        scale = 1.0 / total

        def put(b, part, value):
            at = pl.ds(part * tok, tok)
            if b == 4:
                g_own[h, at] = value
            elif b == Z:
                g_z[h, at] = value
            elif b == X:
                g_x[h, at] = value
            else:
                g_out[b, h, at] = value.astype(jnp.bfloat16)

        out = jnp.zeros((rows, dim), jnp.float32)
        for b in range(5):
            w = p_scr[b] * scale
            p_scr[b] = w
            probs = w.astype(jnp.bfloat16)
            out += dot(probs, chunk(b, h)[tok : 2 * tok, :], 1, 0)
            put(b, 1, dot(probs, do, 0, 0))
        out = out.astype(jnp.bfloat16)
        for w in range(width):
            at = pl.ds(pl.multiple_of((h * width + w) * dim, dim), dim)
            o_ref[:, at] = out[w * tok : (w + 1) * tok]
        delta = jnp.sum(do.astype(jnp.float32) * out.astype(jnp.float32), axis=1, keepdims=True)
        dq = jnp.zeros((rows, dim), jnp.float32)
        for b in range(5):
            dp = dot(do, chunk(b, h)[tok : 2 * tok, :], 1, 1)
            ds = (p_scr[b] * (dp - delta)).astype(jnp.bfloat16)
            dq += dot(ds, chunk(b, h)[:tok, :], 1, 0)
            put(b, 0, FACTOR * dot(ds, q, 0, 0))
        dq_ref[pl.ds(h * width, width)] = (FACTOR * dq).astype(jnp.bfloat16).reshape(width, tok, dim)

    stage_z(0)
    stage_z(1)
    stage_x(0)
    stage_c(0)
    masks()

    @pl.loop(0, heads)
    def _(h):
        @pl.when(h + 2 < heads)
        def _():
            stage_z(h + 2)

        @pl.when(h + 1 < heads)
        def _():
            stage_x(h + 1)

        @pl.when(h > 0)
        def _():
            stage_c(h)

        compute(h)
        gcopy(D, h, core_peer).start()
        gcopy(C, h, core_peer).start()

        @pl.when(h >= 1)
        def _():
            grad_x(h - 1)

        @pl.when(h >= 2)
        def _():
            grad_z(h - 2)

    grad_x(heads - 1)
    grad_z(heads - 2)
    grad_z(heads - 1)

    @pl.loop(0, heads)
    def _(h):
        finish(h)

        @pl.when(has_next)
        def _():
            z_copy(h).wait_send()

        x_copy(h, own_ref).wait_send()
        c_copy(h, own_ref).wait_send()
        d_copy(h).wait_send()
        gcopy(D, h, core_peer).wait_send()
        gcopy(C, h, core_peer).wait_send()
        gcopy(X, h, x_peer).wait_send()

        @pl.when(has_prev)
        def _():
            gcopy(Z, h, me - 4).wait_send()


def attention(q, do, seg, own):
    heads, tok, dim = q.shape
    kv_heads, rows_kv, _ = own.shape
    width = heads // kv_heads
    pairs = heads * tok * tok * 5
    vmem = pl.BlockSpec(memory_space=pltpu.VMEM)
    grad = (kv_heads, 2 * tok, dim)
    return pl.pallas_call(
        functools.partial(attention_kernel, lax.axis_size("seq")),
        in_specs=[vmem] * 4,
        out_specs=[vmem] * 3,
        out_shape=[
            jax.ShapeDtypeStruct((tok, heads * dim), jnp.bfloat16),
            jax.ShapeDtypeStruct((heads, tok, dim), jnp.bfloat16),
            jax.ShapeDtypeStruct(grad, jnp.bfloat16),
        ],
        scratch_shapes=[
            pltpu.VMEM((4,) + own.shape, jnp.bfloat16),
            pltpu.VMEM((5, width * tok, tok), jnp.float32),
            pltpu.VMEM((5, tok, tok), jnp.float32),
            pltpu.VMEM(grad, jnp.float32),
            pltpu.VMEM(grad, jnp.float32),
            pltpu.VMEM(grad, jnp.float32),
            pltpu.VMEM((4,) + grad, jnp.bfloat16),
            pltpu.VMEM((4,) + grad, jnp.bfloat16),
            pltpu.SemaphoreType.DMA((4, kv_heads)),
            pltpu.SemaphoreType.DMA((4, kv_heads)),
            pltpu.SemaphoreType.DMA((4, kv_heads)),
            pltpu.SemaphoreType.DMA((4, kv_heads)),
        ],
        compiler_params=pltpu.CompilerParams(
            vmem_limit_bytes=48 * 2**20, collective_id=0, has_side_effects=True
        ),
        cost_estimate=pl.CostEstimate(
            flops=10 * pairs * dim, bytes_accessed=8 * 2**20, transcendentals=pairs
        ),
        name="attention",
    )(q, do, seg, own)


def pick_kernel(order_ref, held_ref, out_ref):
    for q in range(out_ref.shape[0]):
        out_ref[q] = held_ref[order_ref[q]]


def pick(held, order):
    return pl.pallas_call(
        pick_kernel,
        in_specs=[
            pl.BlockSpec(memory_space=pltpu.SMEM),
            pl.BlockSpec(memory_space=pltpu.VMEM),
        ],
        out_specs=pl.BlockSpec(memory_space=pltpu.VMEM),
        out_shape=jax.ShapeDtypeStruct(held.shape, held.dtype),
        name="pick",
    )(order, held)


def local(queries, keys, values, output_gradient, segment_ids, block_order):
    tok, q_heads, dim = queries.shape
    kv_heads = keys.shape[1]
    seq_count = lax.axis_size("seq")
    head_count = lax.axis_size("head")
    seg = segment_ids.astype(jnp.float32)
    seg_rows = seg.astype(jnp.bfloat16).reshape(tok // dim, dim)
    seg_rows = jnp.pad(seg_rows, ((0, SEG_ROWS - tok // dim), (0, 0)))
    own = jnp.concatenate(
        [
            jnp.moveaxis(keys, 1, 0),
            jnp.moveaxis(values, 1, 0),
            jnp.broadcast_to(seg_rows[None], (kv_heads, SEG_ROWS, dim)),
        ],
        axis=1,
    )
    attended, dq, grads = attention(
        jnp.moveaxis(queries, 1, 0), jnp.moveaxis(output_gradient, 1, 0), seg[:, None], own
    )

    nb = block_order.shape[0] // seq_count
    piece = tok // nb // seq_count
    features = q_heads * dim
    flat = jnp.swapaxes(attended.reshape(nb, seq_count, piece, features), 0, 1)
    spread = lax.all_to_all(flat, "seq", split_axis=0, concat_axis=0, tiled=True)
    ordered = pick(spread.reshape(nb * seq_count, piece, features), block_order)
    delivered = lax.all_to_all(
        ordered.reshape(seq_count, nb, piece, features),
        "seq",
        split_axis=0,
        concat_axis=0,
        tiled=True,
    )
    reordered = jnp.swapaxes(delivered, 0, 1).reshape(head_count, tok // head_count, features)
    halves = lax.all_to_all(reordered, "head", split_axis=0, concat_axis=0, tiled=True)
    relaid = jnp.swapaxes(halves, 0, 1).reshape(tok // head_count, head_count * features)

    grads = jnp.moveaxis(grads.reshape(kv_heads, 2, tok, dim), 0, 2)
    return (relaid, jnp.moveaxis(dq, 0, 1), grads[0], grads[1])


def solution(mesh):
    placed = (
        P("seq", "head", None),
        P("seq", "head", None),
        P("seq", "head", None),
        P("seq", "head", None),
        P("seq"),
        P(),
    )
    return jax.shard_map(
        local,
        mesh=mesh,
        in_specs=placed,
        out_specs=(
            P(("seq", "head"), None),
            P("seq", "head", None),
            P("seq", "head", None),
            P("seq", "head", None),
        ),
        check_vma=False,
    )
```

```python
import functools

import jax
import jax.numpy as jnp
from jax import lax
from jax.experimental import pallas as pl
from jax.experimental.pallas import tpu as pltpu
from jax.sharding import PartitionSpec as P

WINDOW_LENGTH = 1024
QSCALAR = 168
FACTOR = QSCALAR ** (-0.5)
LOG2E = 1.4426950408889634
SEG_ROWS = 16
MESH = pl.DeviceIdType.MESH


def dot(a, b, ca, cb):
    return lax.dot_general(a, b, (((ca,), (cb,)), ((), ())), preferred_element_type=jnp.float32)


def attention_kernel(
    n_seq,
    n_head,
    relay,
    q_ref,
    do_ref,
    seg_ref,
    own_ref,
    order_ref,
    o_ref,
    dq_ref,
    g_ref,
    kv_in,
    p_scr,
    bias,
    g_x,
    g_z,
    g_own,
    g_out,
    g_in,
    send,
    recv,
    g_send,
    g_recv,
    o_out=None,
    held=None,
    picked=None,
    o_send=None,
    o_recv=None,
    r_send=None,
    r_recv=None,
):
    heads, rows_kv, dim = own_ref.shape
    tok = seg_ref.shape[0]
    width = q_ref.shape[0] // heads
    rows = width * tok
    me = lax.axis_index("seq")
    core = lax.rem(me, 2)
    half = lax.rem(me // 2, 2)
    plane = me // 4
    planes = n_seq // 4
    core_peer = me + 1 - 2 * core
    x_peer = me + 2 - 4 * half
    has_prev = plane > 0
    has_next = plane < planes - 1
    Z, X, C, D = 0, 1, 2, 3

    barrier = pltpu.get_barrier_semaphore()
    side = lax.axis_index("head")
    slot = me * n_head + side
    n_dev = n_seq * n_head

    def greet(who, which):
        pl.semaphore_signal(
            barrier, inc=1, device_id={"seq": who, "head": which}, device_id_type=MESH
        )

    if relay:

        @pl.loop(1, n_dev)
        def _(k):
            other = lax.rem(slot + k, n_dev)
            greet(other // n_head, lax.rem(other, n_head))

        pl.semaphore_wait(barrier, n_dev - 1)
    else:
        greet(core_peer, side)
        greet(x_peer, side)

        @pl.when(has_prev)
        def _():
            greet(me - 4, side)

        @pl.when(has_next)
        def _():
            greet(me + 4, side)

        pl.semaphore_wait(barrier, 2 + has_prev.astype(jnp.int32) + has_next.astype(jnp.int32))

    def turn(step, at):
        return lax.rem(step + 2 * at, heads)

    def copy(kind, h, src, who):
        return pltpu.make_async_remote_copy(
            src_ref=src,
            dst_ref=kv_in.at[kind, h],
            send_sem=send.at[kind, h],
            recv_sem=recv.at[kind, h],
            device_id={"seq": who},
            device_id_type=MESH,
        )

    def z_copy(h):
        return copy(Z, h, own_ref.at[h], me + 4)

    def x_copy(h, src):
        return copy(X, h, src.at[h], x_peer)

    def c_copy(h, src):
        return copy(C, h, src.at[h], core_peer)

    def d_copy(h):
        return copy(D, h, kv_in.at[X, h], core_peer)

    @pl.loop(0, heads)
    def _(step):
        h = turn(step, plane)

        @pl.when(has_next)
        def _():
            z_copy(turn(step, plane + 1)).start()

        @pl.when(half == 0)
        def _():
            x_copy(h, own_ref).start()

        @pl.when(core == 0)
        def _():
            c_copy(h, own_ref).start()

        @pl.when(jnp.logical_not(has_prev))
        def _():
            kv_in[Z, h] = jnp.zeros((rows_kv, dim), jnp.bfloat16)

    def stage_z(h):
        @pl.when(has_prev)
        def _():
            copy(Z, h, own_ref.at[h], me - 4).wait_recv()

        @pl.when(half == 1)
        def _():
            x_copy(h, kv_in.at[Z]).start()

        @pl.when(core == 1)
        def _():
            c_copy(h, kv_in.at[Z]).start()

    def stage_x(h):
        x_copy(h, own_ref).wait_recv()
        d_copy(h).start()

    def stage_c(h):
        c_copy(h, own_ref).wait_recv()
        d_copy(h).wait_recv()

    def gcopy(kind, h, who):
        return pltpu.make_async_remote_copy(
            src_ref=g_out.at[kind, h],
            dst_ref=g_in.at[kind, h],
            send_sem=g_send.at[kind, h],
            recv_sem=g_recv.at[kind, h],
            device_id={"seq": who},
            device_id_type=MESH,
        )

    def grad_x(h):
        gcopy(D, h, core_peer).wait_recv()
        total = g_x[h] + g_in[D, h].astype(jnp.float32)
        g_out[X, h] = total.astype(jnp.bfloat16)
        gcopy(X, h, x_peer).start()

    def grad_z(h):
        gcopy(C, h, core_peer).wait_recv()
        gcopy(X, h, x_peer).wait_recv()
        from_c = g_in[C, h].astype(jnp.float32)
        from_x = g_in[X, h].astype(jnp.float32)
        zero = jnp.zeros_like(from_c)
        back = g_z[h] + jnp.where(core == 1, from_c, zero) + jnp.where(half == 1, from_x, zero)
        g_out[Z, h] = back.astype(jnp.bfloat16)
        g_own[h] = g_own[h] + jnp.where(core == 0, from_c, zero) + jnp.where(half == 0, from_x, zero)

        @pl.when(has_prev)
        def _():
            gcopy(Z, h, me - 4).start()

    def finish(h):
        @pl.when(has_next)
        def _():
            gcopy(Z, h, me + 4).wait_recv()
            g_ref[h] = (g_own[h] + g_in[Z, h].astype(jnp.float32)).astype(jnp.bfloat16)

        @pl.when(jnp.logical_not(has_next))
        def _():
            g_ref[h] = g_own[h].astype(jnp.bfloat16)

    spans = (4, 2, 3 - 2 * core, 1 + 2 * core, 0)

    def chunk(b, h):
        return own_ref.at[h] if b == 4 else kv_in.at[b, h]

    def masks():
        gap = lax.broadcasted_iota(jnp.int32, (tok, tok), 0) - lax.broadcasted_iota(
            jnp.int32, (tok, tok), 1
        )
        seg_q = seg_ref[...]
        for b in range(5):
            segs = chunk(b, turn(0, plane))[2 * tok :, :].astype(jnp.float32)
            seg_k = jnp.concatenate([segs[r : r + 1] for r in range(tok // dim)], axis=1)
            far = gap + spans[b] * tok
            near = jnp.where(me >= spans[b], WINDOW_LENGTH, -1)
            allowed = (far >= 0) & (far < near) & (seg_q == seg_k)
            bias[b] = jnp.where(allowed, 0.0, -jnp.inf)

    def ocopy(head, source):
        return pltpu.make_async_remote_copy(
            src_ref=o_out.at[head],
            dst_ref=held.at[source],
            send_sem=o_send.at[head],
            recv_sem=o_recv.at[source],
            device_id={"seq": head},
            device_id_type=MESH,
        )

    def send_out(head, part):
        part = part.reshape(o_out.shape[1:])

        @pl.when(head == me)
        def _():
            held[me] = part

        @pl.when(head != me)
        def _():
            o_out[head] = part
            ocopy(head, me).start()

    def rcopy(block, source):
        column = lax.rem(source, n_head) * n_seq + source // n_head
        return pltpu.make_async_remote_copy(
            src_ref=picked.at[block],
            dst_ref=o_ref.at[:, pl.ds(pl.multiple_of(column * dim, dim), dim)],
            send_sem=r_send.at[block],
            recv_sem=r_recv.at[source],
            device_id={"seq": block // n_head, "head": lax.rem(block, n_head)},
            device_id_type=MESH,
        )

    def pick_and_send():
        @pl.loop(1, n_seq)
        def _(k):
            other = lax.rem(me + k, n_seq)
            ocopy(other, other).wait_recv()

        per = n_dev // n_seq

        @pl.loop(1, n_dev)
        def _(k):
            block = lax.rem(slot + k, n_dev)
            source = order_ref[block]
            picked[block] = held[source // per, lax.rem(source, per)]
            rcopy(block, slot).start()

        source = order_ref[slot]
        column = (side * n_seq + me) * dim
        o_ref[:, pl.ds(pl.multiple_of(column, dim), dim)] = held[source // per, lax.rem(source, per)]

    def settle():
        @pl.loop(1, n_seq)
        def _(k):
            ocopy(lax.rem(me + k, n_seq), me).wait_send()

        @pl.loop(1, n_dev)
        def _(k):
            other = lax.rem(slot + k, n_dev)
            rcopy(other, slot).wait_send()
            rcopy(other, other).wait_recv()

    def compute(h):
        q = q_ref[pl.ds(h * width, width)].reshape(rows, dim)
        do = do_ref[pl.ds(h * width, width)].reshape(rows, dim)
        top = None
        for b in range(5):
            s = dot(q, chunk(b, h)[:tok, :], 1, 1).reshape(width, tok, tok)
            s = (s + bias[b][None]).reshape(rows, tok)
            p_scr[b] = s
            m = jnp.max(s, axis=1, keepdims=True)
            top = m if top is None else jnp.maximum(top, m)
        total = jnp.zeros((rows, 1), jnp.float32)
        for b in range(5):
            p = jnp.exp2((p_scr[b] - top) * (FACTOR * LOG2E))
            p_scr[b] = p
            total += jnp.sum(p, axis=1, keepdims=True)
        scale = 1.0 / total

        def put(b, part, value):
            at = pl.ds(part * tok, tok)
            if b == 4:
                g_own[h, at] = value
            elif b == Z:
                g_z[h, at] = value
            elif b == X:
                g_x[h, at] = value
            else:
                g_out[b, h, at] = value.astype(jnp.bfloat16)

        out = jnp.zeros((rows, dim), jnp.float32)
        for b in range(5):
            w = p_scr[b] * scale
            p_scr[b] = w
            probs = w.astype(jnp.bfloat16)
            out += dot(probs, chunk(b, h)[tok : 2 * tok, :], 1, 0)
            put(b, 1, dot(probs, do, 0, 0))
        out = out.astype(jnp.bfloat16)
        for w in range(width):
            head = h * width + w
            part = out[w * tok : (w + 1) * tok]
            if relay:
                send_out(head, part)
            else:
                o_ref[:, pl.ds(pl.multiple_of(head * dim, dim), dim)] = part
        delta = jnp.sum(do.astype(jnp.float32) * out.astype(jnp.float32), axis=1, keepdims=True)
        dq = jnp.zeros((rows, dim), jnp.float32)
        for b in range(5):
            dp = dot(do, chunk(b, h)[tok : 2 * tok, :], 1, 1)
            ds = (p_scr[b] * (dp - delta)).astype(jnp.bfloat16)
            dq += dot(ds, chunk(b, h)[:tok, :], 1, 0)
            put(b, 0, FACTOR * dot(ds, q, 0, 0))
        dq_ref[pl.ds(h * width, width)] = (FACTOR * dq).astype(jnp.bfloat16).reshape(width, tok, dim)

    stage_z(turn(0, plane))
    stage_z(turn(1, plane))
    stage_x(turn(0, plane))
    stage_c(turn(0, plane))
    masks()

    @pl.loop(0, heads)
    def _(step):
        h = turn(step, plane)

        @pl.when(step + 2 < heads)
        def _():
            stage_z(turn(step + 2, plane))

        @pl.when(step + 1 < heads)
        def _():
            stage_x(turn(step + 1, plane))

        @pl.when(step > 0)
        def _():
            stage_c(h)

        compute(h)
        gcopy(D, h, core_peer).start()
        gcopy(C, h, core_peer).start()

        @pl.when(step >= 1)
        def _():
            grad_x(turn(step + heads - 1, plane))

        @pl.when(step >= 2)
        def _():
            grad_z(turn(step + heads - 2, plane))

    grad_x(turn(heads - 1, plane))
    grad_z(turn(heads - 2, plane))
    grad_z(turn(heads - 1, plane))
    if relay:
        pick_and_send()

    @pl.loop(0, heads)
    def _(step):
        h = turn(step, plane)
        finish(h)

        @pl.when(has_next)
        def _():
            z_copy(h).wait_send()

        x_copy(h, own_ref).wait_send()
        c_copy(h, own_ref).wait_send()
        d_copy(h).wait_send()
        gcopy(D, h, core_peer).wait_send()
        gcopy(C, h, core_peer).wait_send()
        gcopy(X, h, x_peer).wait_send()

        @pl.when(has_prev)
        def _():
            gcopy(Z, h, me - 4).wait_send()

    if relay:
        settle()


def attention(q, do, seg, own, order, relay):
    heads, tok, dim = q.shape
    kv_heads, rows_kv, _ = own.shape
    width = heads // kv_heads
    pairs = heads * tok * tok * 5
    vmem = pl.BlockSpec(memory_space=pltpu.VMEM)
    grad = (kv_heads, 2 * tok, dim)
    n_seq, n_head = lax.axis_size("seq"), lax.axis_size("head")
    blocks = order.shape[0]
    out_shape = (tok // n_head, n_head * heads * dim) if relay else (tok, heads * dim)
    rows_out = tok * n_seq // blocks
    relay_scratch = [
        pltpu.VMEM((heads, blocks // n_seq, rows_out, dim), jnp.bfloat16),
        pltpu.VMEM((n_seq, blocks // n_seq, rows_out, dim), jnp.bfloat16),
        pltpu.VMEM((blocks, rows_out, dim), jnp.bfloat16),
        pltpu.SemaphoreType.DMA((n_seq,)),
        pltpu.SemaphoreType.DMA((n_seq,)),
        pltpu.SemaphoreType.DMA((blocks,)),
        pltpu.SemaphoreType.DMA((blocks,)),
    ]
    return pl.pallas_call(
        functools.partial(attention_kernel, n_seq, n_head, relay),
        in_specs=[vmem] * 4 + [pl.BlockSpec(memory_space=pltpu.SMEM)],
        out_specs=[vmem] * 3,
        out_shape=[
            jax.ShapeDtypeStruct(out_shape, jnp.bfloat16),
            jax.ShapeDtypeStruct((heads, tok, dim), jnp.bfloat16),
            jax.ShapeDtypeStruct(grad, jnp.bfloat16),
        ],
        scratch_shapes=[
            pltpu.VMEM((4,) + own.shape, jnp.bfloat16),
            pltpu.VMEM((5, width * tok, tok), jnp.float32),
            pltpu.VMEM((5, tok, tok), jnp.float32),
            pltpu.VMEM(grad, jnp.float32),
            pltpu.VMEM(grad, jnp.float32),
            pltpu.VMEM(grad, jnp.float32),
            pltpu.VMEM((4,) + grad, jnp.bfloat16),
            pltpu.VMEM((4,) + grad, jnp.bfloat16),
            pltpu.SemaphoreType.DMA((4, kv_heads)),
            pltpu.SemaphoreType.DMA((4, kv_heads)),
            pltpu.SemaphoreType.DMA((4, kv_heads)),
            pltpu.SemaphoreType.DMA((4, kv_heads)),
        ]
        + (relay_scratch if relay else []),
        compiler_params=pltpu.CompilerParams(
            vmem_limit_bytes=48 * 2**20, collective_id=0, has_side_effects=True
        ),
        cost_estimate=pl.CostEstimate(
            flops=10 * pairs * dim, bytes_accessed=8 * 2**20, transcendentals=pairs
        ),
        name="attention",
    )(q, do, seg, own, order)


def pick_kernel(order_ref, held_ref, out_ref):
    for q in range(out_ref.shape[0]):
        out_ref[q] = held_ref[order_ref[q]]


def pick(held, order):
    return pl.pallas_call(
        pick_kernel,
        in_specs=[
            pl.BlockSpec(memory_space=pltpu.SMEM),
            pl.BlockSpec(memory_space=pltpu.VMEM),
        ],
        out_specs=pl.BlockSpec(memory_space=pltpu.VMEM),
        out_shape=jax.ShapeDtypeStruct(held.shape, held.dtype),
        name="pick",
    )(order, held)


def local(queries, keys, values, output_gradient, segment_ids, block_order):
    tok, q_heads, dim = queries.shape
    kv_heads = keys.shape[1]
    seq_count = lax.axis_size("seq")
    head_count = lax.axis_size("head")
    seg = segment_ids.astype(jnp.float32)
    seg_rows = seg.astype(jnp.bfloat16).reshape(tok // dim, dim)
    seg_rows = jnp.pad(seg_rows, ((0, SEG_ROWS - tok // dim), (0, 0)))
    own = jnp.concatenate(
        [
            jnp.moveaxis(keys, 1, 0),
            jnp.moveaxis(values, 1, 0),
            jnp.broadcast_to(seg_rows[None], (kv_heads, SEG_ROWS, dim)),
        ],
        axis=1,
    )
    relay = q_heads == seq_count and block_order.shape[0] == seq_count * head_count
    attended, dq, grads = attention(
        jnp.moveaxis(queries, 1, 0),
        jnp.moveaxis(output_gradient, 1, 0),
        seg[:, None],
        own,
        block_order,
        relay,
    )
    grads = jnp.moveaxis(grads.reshape(kv_heads, 2, tok, dim), 0, 2)
    dq = jnp.moveaxis(dq, 0, 1)
    if relay:
        return (attended, dq, grads[0], grads[1])

    nb = block_order.shape[0] // seq_count
    piece = tok // nb // seq_count
    features = q_heads * dim
    flat = jnp.swapaxes(attended.reshape(nb, seq_count, piece, features), 0, 1)
    spread = lax.all_to_all(flat, "seq", split_axis=0, concat_axis=0, tiled=True)
    ordered = pick(spread.reshape(nb * seq_count, piece, features), block_order)
    delivered = lax.all_to_all(
        ordered.reshape(seq_count, nb, piece, features),
        "seq",
        split_axis=0,
        concat_axis=0,
        tiled=True,
    )
    reordered = jnp.swapaxes(delivered, 0, 1).reshape(head_count, tok // head_count, features)
    halves = lax.all_to_all(reordered, "head", split_axis=0, concat_axis=0, tiled=True)
    relaid = jnp.swapaxes(halves, 0, 1).reshape(tok // head_count, head_count * features)

    return (relaid, dq, grads[0], grads[1])


def solution(mesh):
    placed = (
        P("seq", "head", None),
        P("seq", "head", None),
        P("seq", "head", None),
        P("seq", "head", None),
        P("seq"),
        P(),
    )
    return jax.shard_map(
        local,
        mesh=mesh,
        in_specs=placed,
        out_specs=(
            P(("seq", "head"), None),
            P("seq", "head", None),
            P("seq", "head", None),
            P("seq", "head", None),
        ),
        check_vma=False,
    )
```

```python
import functools

import jax
import jax.numpy as jnp
from jax import lax
from jax.experimental import pallas as pl
from jax.experimental.pallas import tpu as pltpu
from jax.sharding import PartitionSpec as P

WINDOW_LENGTH = 1024
QSCALAR = 168
FACTOR = QSCALAR ** (-0.5)
LOG2E = 1.4426950408889634
SEG_ROWS = 16
MESH = pl.DeviceIdType.MESH


def dot(a, b, ca, cb):
    return lax.dot_general(a, b, (((ca,), (cb,)), ((), ())), preferred_element_type=jnp.float32)


def attention_kernel(
    n_seq,
    n_head,
    relay,
    q_ref,
    do_ref,
    seg_ref,
    own_ref,
    order_ref,
    o_ref,
    dq_ref,
    g_ref,
    kv_in,
    p_scr,
    bias,
    g_x,
    g_z,
    g_own,
    g_out,
    g_in,
    send,
    recv,
    g_send,
    g_recv,
    o_out=None,
    held=None,
    picked=None,
    o_send=None,
    o_recv=None,
    r_send=None,
    r_recv=None,
):
    heads, rows_kv, dim = own_ref.shape
    tok = seg_ref.shape[0]
    width = q_ref.shape[0] // heads
    rows = width * tok
    me = lax.axis_index("seq")
    core = lax.rem(me, 2)
    half = lax.rem(me // 2, 2)
    plane = me // 4
    planes = n_seq // 4
    core_peer = me + 1 - 2 * core
    x_peer = me + 2 - 4 * half
    has_prev = plane > 0
    has_next = plane < planes - 1
    Z, X, C, D = 0, 1, 2, 3

    barrier = pltpu.get_barrier_semaphore()
    side = lax.axis_index("head")
    slot = me * n_head + side
    n_dev = n_seq * n_head

    def greet(who, which):
        pl.semaphore_signal(
            barrier, inc=1, device_id={"seq": who, "head": which}, device_id_type=MESH
        )

    if relay:

        @pl.loop(1, n_dev)
        def _(k):
            other = lax.rem(slot + k, n_dev)
            greet(other // n_head, lax.rem(other, n_head))

        pl.semaphore_wait(barrier, n_dev - 1)
    else:
        greet(core_peer, side)
        greet(x_peer, side)

        @pl.when(has_prev)
        def _():
            greet(me - 4, side)

        @pl.when(has_next)
        def _():
            greet(me + 4, side)

        pl.semaphore_wait(barrier, 2 + has_prev.astype(jnp.int32) + has_next.astype(jnp.int32))

    def turn(step, at):
        return lax.rem(step + 2 * at, heads)

    def copy(kind, h, src, who):
        return pltpu.make_async_remote_copy(
            src_ref=src,
            dst_ref=kv_in.at[kind, h],
            send_sem=send.at[kind, h],
            recv_sem=recv.at[kind, h],
            device_id={"seq": who},
            device_id_type=MESH,
        )

    def z_copy(h):
        return copy(Z, h, own_ref.at[h], me + 4)

    def x_copy(h, src):
        return copy(X, h, src.at[h], x_peer)

    def c_copy(h, src):
        return copy(C, h, src.at[h], core_peer)

    def d_copy(h):
        return copy(D, h, kv_in.at[X, h], core_peer)

    @pl.loop(0, heads)
    def _(step):
        h = turn(step, plane)

        @pl.when(has_next)
        def _():
            z_copy(turn(step, plane + 1)).start()

        @pl.when(half == 0)
        def _():
            x_copy(h, own_ref).start()

        @pl.when(core == 0)
        def _():
            c_copy(h, own_ref).start()

        @pl.when(jnp.logical_not(has_prev))
        def _():
            kv_in[Z, h] = jnp.zeros((rows_kv, dim), jnp.bfloat16)

    def stage_z(h):
        @pl.when(has_prev)
        def _():
            copy(Z, h, own_ref.at[h], me - 4).wait_recv()

        @pl.when(half == 1)
        def _():
            x_copy(h, kv_in.at[Z]).start()

        @pl.when(core == 1)
        def _():
            c_copy(h, kv_in.at[Z]).start()

    def stage_x(h):
        x_copy(h, own_ref).wait_recv()
        d_copy(h).start()

    def stage_c(h):
        c_copy(h, own_ref).wait_recv()
        d_copy(h).wait_recv()

    def gcopy(kind, h, who):
        return pltpu.make_async_remote_copy(
            src_ref=g_out.at[kind, h],
            dst_ref=g_in.at[kind, h],
            send_sem=g_send.at[kind, h],
            recv_sem=g_recv.at[kind, h],
            device_id={"seq": who},
            device_id_type=MESH,
        )

    def grad_x(h):
        gcopy(D, h, core_peer).wait_recv()
        total = g_x[h] + g_in[D, h].astype(jnp.float32)
        g_out[X, h] = total.astype(jnp.bfloat16)
        gcopy(X, h, x_peer).start()

    def grad_z(h):
        gcopy(C, h, core_peer).wait_recv()
        gcopy(X, h, x_peer).wait_recv()
        from_c = g_in[C, h].astype(jnp.float32)
        from_x = g_in[X, h].astype(jnp.float32)
        zero = jnp.zeros_like(from_c)
        back = g_z[h] + jnp.where(core == 1, from_c, zero) + jnp.where(half == 1, from_x, zero)
        g_out[Z, h] = back.astype(jnp.bfloat16)
        g_own[h] = g_own[h] + jnp.where(core == 0, from_c, zero) + jnp.where(half == 0, from_x, zero)

        @pl.when(has_prev)
        def _():
            gcopy(Z, h, me - 4).start()

    def finish(h):
        @pl.when(has_next)
        def _():
            gcopy(Z, h, me + 4).wait_recv()
            g_ref[h] = (g_own[h] + g_in[Z, h].astype(jnp.float32)).astype(jnp.bfloat16)

        @pl.when(jnp.logical_not(has_next))
        def _():
            g_ref[h] = g_own[h].astype(jnp.bfloat16)

    spans = (4, 2, 3 - 2 * core, 1 + 2 * core, 0)

    def chunk(b, h):
        return own_ref.at[h] if b == 4 else kv_in.at[b, h]

    def masks():
        gap = lax.broadcasted_iota(jnp.int32, (tok, tok), 0) - lax.broadcasted_iota(
            jnp.int32, (tok, tok), 1
        )
        seg_q = seg_ref[...]
        for b in range(5):
            segs = chunk(b, turn(0, plane))[2 * tok :, :].astype(jnp.float32)
            seg_k = jnp.concatenate([segs[r : r + 1] for r in range(tok // dim)], axis=1)
            far = gap + spans[b] * tok
            near = jnp.where(me >= spans[b], WINDOW_LENGTH, -1)
            allowed = (far >= 0) & (far < near) & (seg_q == seg_k)
            bias[b] = jnp.where(allowed, 0.0, -jnp.inf)

    def ocopy(head, source):
        return pltpu.make_async_remote_copy(
            src_ref=o_out.at[head],
            dst_ref=held.at[source],
            send_sem=o_send.at[head],
            recv_sem=o_recv.at[source],
            device_id={"seq": head},
            device_id_type=MESH,
        )

    def send_out(head, part):
        part = part.reshape(o_out.shape[1:])

        @pl.when(head == me)
        def _():
            held[me] = part

        @pl.when(head != me)
        def _():
            o_out[head] = part
            ocopy(head, me).start()

    def rcopy(block, source):
        column = lax.rem(source, n_head) * n_seq + source // n_head
        return pltpu.make_async_remote_copy(
            src_ref=picked.at[block],
            dst_ref=o_ref.at[:, pl.ds(pl.multiple_of(column * dim, dim), dim)],
            send_sem=r_send.at[block],
            recv_sem=r_recv.at[source],
            device_id={"seq": block // n_head, "head": lax.rem(block, n_head)},
            device_id_type=MESH,
        )

    def pick_and_send():
        @pl.loop(1, n_seq)
        def _(k):
            other = lax.rem(me + k, n_seq)
            ocopy(other, other).wait_recv()

        per = n_dev // n_seq

        @pl.loop(1, n_dev)
        def _(k):
            block = lax.rem(slot + k, n_dev)
            source = order_ref[block]
            picked[block] = held[source // per, lax.rem(source, per)]
            rcopy(block, slot).start()

        source = order_ref[slot]
        column = (side * n_seq + me) * dim
        o_ref[:, pl.ds(pl.multiple_of(column, dim), dim)] = held[source // per, lax.rem(source, per)]

    def settle():
        @pl.loop(1, n_seq)
        def _(k):
            ocopy(lax.rem(me + k, n_seq), me).wait_send()

        @pl.loop(1, n_dev)
        def _(k):
            other = lax.rem(slot + k, n_dev)
            rcopy(other, slot).wait_send()
            rcopy(other, other).wait_recv()

    def compute(h):
        q = q_ref[pl.ds(h * width, width)].reshape(rows, dim)
        do = do_ref[pl.ds(h * width, width)].reshape(rows, dim)
        top = None
        for b in range(5):
            s = dot(q, chunk(b, h)[:tok, :], 1, 1).reshape(width, tok, tok)
            s = (s + bias[b][None]).reshape(rows, tok)
            p_scr[b] = s
            m = jnp.max(s, axis=1, keepdims=True)
            top = m if top is None else jnp.maximum(top, m)
        total = jnp.zeros((rows, 1), jnp.float32)
        for b in range(5):
            p = jnp.exp2((p_scr[b] - top) * (FACTOR * LOG2E))
            p_scr[b] = p
            total += jnp.sum(p, axis=1, keepdims=True)
        scale = 1.0 / total

        def put(b, part, value):
            at = pl.ds(part * tok, tok)
            if b == 4:
                g_own[h, at] = value
            elif b == Z:
                g_z[h, at] = value
            elif b == X:
                g_x[h, at] = value
            else:
                g_out[b, h, at] = value.astype(jnp.bfloat16)

        out = jnp.zeros((rows, dim), jnp.float32)
        for b in range(5):
            w = p_scr[b] * scale
            p_scr[b] = w
            probs = w.astype(jnp.bfloat16)
            out += dot(probs, chunk(b, h)[tok : 2 * tok, :], 1, 0)
            put(b, 1, dot(probs, do, 0, 0))
        out = out.astype(jnp.bfloat16)
        for w in range(width):
            head = h * width + w
            part = out[w * tok : (w + 1) * tok]
            if relay:
                send_out(head, part)
            else:
                o_ref[:, pl.ds(pl.multiple_of(head * dim, dim), dim)] = part
        delta = jnp.sum(do.astype(jnp.float32) * out.astype(jnp.float32), axis=1, keepdims=True)
        dq = jnp.zeros((rows, dim), jnp.float32)
        for b in range(5):
            dp = dot(do, chunk(b, h)[tok : 2 * tok, :], 1, 1)
            ds = (p_scr[b] * (dp - delta)).astype(jnp.bfloat16)
            dq += dot(ds, chunk(b, h)[:tok, :], 1, 0)
            put(b, 0, FACTOR * dot(ds, q, 0, 0))
        dq_ref[pl.ds(h * width, width)] = (FACTOR * dq).astype(jnp.bfloat16).reshape(width, tok, dim)

    stage_z(turn(0, plane))
    stage_z(turn(1, plane))
    stage_x(turn(0, plane))
    stage_c(turn(0, plane))
    masks()

    @pl.loop(0, heads)
    def _(step):
        h = turn(step, plane)

        @pl.when(step + 2 < heads)
        def _():
            stage_z(turn(step + 2, plane))

        @pl.when(step + 1 < heads)
        def _():
            stage_x(turn(step + 1, plane))

        @pl.when(step > 0)
        def _():
            stage_c(h)

        compute(h)
        gcopy(D, h, core_peer).start()
        gcopy(C, h, core_peer).start()

        @pl.when(step >= 1)
        def _():
            grad_x(turn(step + heads - 1, plane))

        @pl.when(step >= 2)
        def _():
            grad_z(turn(step + heads - 2, plane))

    grad_x(turn(heads - 1, plane))
    grad_z(turn(heads - 2, plane))
    if relay:
        pick_and_send()
    grad_z(turn(heads - 1, plane))

    @pl.loop(0, heads)
    def _(step):
        h = turn(step, plane)
        finish(h)

        @pl.when(has_next)
        def _():
            z_copy(h).wait_send()

        x_copy(h, own_ref).wait_send()
        c_copy(h, own_ref).wait_send()
        d_copy(h).wait_send()
        gcopy(D, h, core_peer).wait_send()
        gcopy(C, h, core_peer).wait_send()
        gcopy(X, h, x_peer).wait_send()

        @pl.when(has_prev)
        def _():
            gcopy(Z, h, me - 4).wait_send()

    if relay:
        settle()


def attention(q, do, seg, own, order, relay):
    heads, tok, dim = q.shape
    kv_heads, rows_kv, _ = own.shape
    width = heads // kv_heads
    pairs = heads * tok * tok * 5
    vmem = pl.BlockSpec(memory_space=pltpu.VMEM)
    grad = (kv_heads, 2 * tok, dim)
    n_seq, n_head = lax.axis_size("seq"), lax.axis_size("head")
    blocks = order.shape[0]
    out_shape = (tok // n_head, n_head * heads * dim) if relay else (tok, heads * dim)
    rows_out = tok * n_seq // blocks
    relay_scratch = [
        pltpu.VMEM((heads, blocks // n_seq, rows_out, dim), jnp.bfloat16),
        pltpu.VMEM((n_seq, blocks // n_seq, rows_out, dim), jnp.bfloat16),
        pltpu.VMEM((blocks, rows_out, dim), jnp.bfloat16),
        pltpu.SemaphoreType.DMA((n_seq,)),
        pltpu.SemaphoreType.DMA((n_seq,)),
        pltpu.SemaphoreType.DMA((blocks,)),
        pltpu.SemaphoreType.DMA((blocks,)),
    ]
    return pl.pallas_call(
        functools.partial(attention_kernel, n_seq, n_head, relay),
        in_specs=[vmem] * 4 + [pl.BlockSpec(memory_space=pltpu.SMEM)],
        out_specs=[vmem] * 3,
        out_shape=[
            jax.ShapeDtypeStruct(out_shape, jnp.bfloat16),
            jax.ShapeDtypeStruct((heads, tok, dim), jnp.bfloat16),
            jax.ShapeDtypeStruct(grad, jnp.bfloat16),
        ],
        scratch_shapes=[
            pltpu.VMEM((4,) + own.shape, jnp.bfloat16),
            pltpu.VMEM((5, width * tok, tok), jnp.float32),
            pltpu.VMEM((5, tok, tok), jnp.float32),
            pltpu.VMEM(grad, jnp.float32),
            pltpu.VMEM(grad, jnp.float32),
            pltpu.VMEM(grad, jnp.float32),
            pltpu.VMEM((4,) + grad, jnp.bfloat16),
            pltpu.VMEM((4,) + grad, jnp.bfloat16),
            pltpu.SemaphoreType.DMA((4, kv_heads)),
            pltpu.SemaphoreType.DMA((4, kv_heads)),
            pltpu.SemaphoreType.DMA((4, kv_heads)),
            pltpu.SemaphoreType.DMA((4, kv_heads)),
        ]
        + (relay_scratch if relay else []),
        compiler_params=pltpu.CompilerParams(
            vmem_limit_bytes=48 * 2**20, collective_id=0, has_side_effects=True
        ),
        cost_estimate=pl.CostEstimate(
            flops=10 * pairs * dim, bytes_accessed=8 * 2**20, transcendentals=pairs
        ),
        name="attention",
    )(q, do, seg, own, order)


def pick_kernel(order_ref, held_ref, out_ref):
    for q in range(out_ref.shape[0]):
        out_ref[q] = held_ref[order_ref[q]]


def pick(held, order):
    return pl.pallas_call(
        pick_kernel,
        in_specs=[
            pl.BlockSpec(memory_space=pltpu.SMEM),
            pl.BlockSpec(memory_space=pltpu.VMEM),
        ],
        out_specs=pl.BlockSpec(memory_space=pltpu.VMEM),
        out_shape=jax.ShapeDtypeStruct(held.shape, held.dtype),
        name="pick",
    )(order, held)


def local(queries, keys, values, output_gradient, segment_ids, block_order):
    tok, q_heads, dim = queries.shape
    kv_heads = keys.shape[1]
    seq_count = lax.axis_size("seq")
    head_count = lax.axis_size("head")
    seg = segment_ids.astype(jnp.float32)
    seg_rows = seg.astype(jnp.bfloat16).reshape(tok // dim, dim)
    seg_rows = jnp.pad(seg_rows, ((0, SEG_ROWS - tok // dim), (0, 0)))
    own = jnp.concatenate(
        [
            jnp.moveaxis(keys, 1, 0),
            jnp.moveaxis(values, 1, 0),
            jnp.broadcast_to(seg_rows[None], (kv_heads, SEG_ROWS, dim)),
        ],
        axis=1,
    )
    relay = q_heads == seq_count and block_order.shape[0] == seq_count * head_count
    attended, dq, grads = attention(
        jnp.moveaxis(queries, 1, 0),
        jnp.moveaxis(output_gradient, 1, 0),
        seg[:, None],
        own,
        block_order,
        relay,
    )
    grads = jnp.moveaxis(grads.reshape(kv_heads, 2, tok, dim), 0, 2)
    dq = jnp.moveaxis(dq, 0, 1)
    if relay:
        return (attended, dq, grads[0], grads[1])

    nb = block_order.shape[0] // seq_count
    piece = tok // nb // seq_count
    features = q_heads * dim
    flat = jnp.swapaxes(attended.reshape(nb, seq_count, piece, features), 0, 1)
    spread = lax.all_to_all(flat, "seq", split_axis=0, concat_axis=0, tiled=True)
    ordered = pick(spread.reshape(nb * seq_count, piece, features), block_order)
    delivered = lax.all_to_all(
        ordered.reshape(seq_count, nb, piece, features),
        "seq",
        split_axis=0,
        concat_axis=0,
        tiled=True,
    )
    reordered = jnp.swapaxes(delivered, 0, 1).reshape(head_count, tok // head_count, features)
    halves = lax.all_to_all(reordered, "head", split_axis=0, concat_axis=0, tiled=True)
    relaid = jnp.swapaxes(halves, 0, 1).reshape(tok // head_count, head_count * features)

    return (relaid, dq, grads[0], grads[1])


def solution(mesh):
    placed = (
        P("seq", "head", None),
        P("seq", "head", None),
        P("seq", "head", None),
        P("seq", "head", None),
        P("seq"),
        P(),
    )
    return jax.shard_map(
        local,
        mesh=mesh,
        in_specs=placed,
        out_specs=(
            P(("seq", "head"), None),
            P("seq", "head", None),
            P("seq", "head", None),
            P("seq", "head", None),
        ),
        check_vma=False,
    )
```
